32 devices in a mesh: seq: 16 (over z, y, x), chan: 2 (over core).
Axes of the slice: x: 2, y: 2, z: 4, core: 2. Of those that a mesh axis runs over, the one named last changes fastest.
Arguments:
- hyena_gate: bfloat16 [8192, 4096], P('seq', 'chan'), may hold values from -6 to 6
- hyena_key: bfloat16 [8192, 4096], P('seq', 'chan'), may hold values from -6 to 6
- hyena_value: bfloat16 [8192, 4096], P('seq', 'chan'), may hold values from -6 to 6
- long_filter: bfloat16 [8192, 4096], P('seq', 'chan'), may hold values from -0.0625 to 0.0625
- skip_weight: float32 [4096], P('chan'), may hold values from -4 to 4
- attn_query: bfloat16 [8192, 8, 1024], P('seq', 'chan'), may hold values from -4.5 to 4.5
- attn_keys: bfloat16 [8192, 1024], P('seq', 'chan'), may hold values from -4.5 to 4.5
- attn_values: bfloat16 [8192, 1024], P('seq', 'chan'), may hold values from -6 to 6
Outputs:
- hyena_out: bfloat16 [8192, 4096], P('seq', 'chan')
- attn_out: bfloat16 [8192, 8, 1024], P('seq', 'chan')
- attn_lse: float32 [8, 8, 8192], P('chan', None, 'seq')
The draws below stay inside these ranges and needn't reach their ends.
All inputs are finite; a program needn't handle non-finite values.
Results may differ from the reference program's by a relative error of at most 0.0045.
Values may be sent and summed in bfloat16 or wider, within the bound.
A program may use at most 192 MiB of HBM per device.

```python
import math
import jax
import jax.numpy as jnp
from jax import lax

C = 4096
KVH = 8
GROUP = 8
HD = 128
TOK_DEV = 512
TOKENS = 8192
N_SEQ = 16


def draw_attn_query(key, part):
    key = jax.random.fold_in(key, 1)
    drawn = jnp.clip(jax.random.normal(key, (TOKENS, GROUP, KVH * HD), jnp.float32), -4.5, 4.5)
    return drawn.astype(jnp.bfloat16)


def draw_attn_keys(key, part):
    key = jax.random.fold_in(key, 2)
    drawn = jnp.clip(jax.random.normal(key, (TOKENS, KVH * HD), jnp.float32), -4.5, 4.5)
    return drawn.astype(jnp.bfloat16)


def shard_levels(rng, shape, split, low, largest):
    level, own = 1.0, jax.random.fold_in(rng, 6)
    for axis_at, parts in split:
        steps = jnp.exp(jax.random.uniform(jax.random.fold_in(own, axis_at), (parts,), jnp.float32, low / len(split), largest / len(split)))
        level = level * jnp.repeat(steps, shape[axis_at] // parts).reshape([-1 if axis == axis_at else 1 for axis in range(len(shape))])
    return level


def centred(key, extent, deviation, reach, cuts=(), held_as=jnp.bfloat16):
    values = deviation * jax.random.normal(key, extent, jnp.float32)
    if cuts:
        values = values * shard_levels(key, extent, cuts, -0.22, 0.18)
    return jnp.clip(values, -reach, reach).astype(held_as)


def setup_inputs(seed: int = 0) -> dict:
    seeds = jax.random.split(jax.random.key(seed), 9)
    return {
        "hyena_gate": centred(seeds[0], (TOKENS, C), 1.0, 6.0, ((0, 16), (1, 2))),
        "hyena_key": centred(seeds[1], (TOKENS, C), 1.0, 6.0, ((0, 16), (1, 2))),
        "hyena_value": centred(seeds[2], (TOKENS, C), 1.0, 6.0, ((0, 16), (1, 2))),
        "long_filter": centred(seeds[3], (TOKENS, C), TOKENS ** -0.5, 0.0625, ((0, 16), (1, 2))),
        "skip_weight": centred(seeds[4], (C,), 1.0, 4.0, ((0, 2),), jnp.float32),
        "attn_query": draw_attn_query(jax.random.fold_in(seeds[8], 71), 0),
        "attn_keys": draw_attn_keys(jax.random.fold_in(seeds[8], 71), 0),
        "attn_values": centred(seeds[7], (TOKENS, KVH * HD), 1.0, 6.0, ((0, 16), (1, 2))),
    }


def long_conv(signal, kernel):
    chan_block = math.gcd(C, 256)
    block_count = C // chan_block

    def regroup(array):
        return array.reshape(TOKENS, block_count, chan_block).transpose(1, 0, 2)

    def convolve(pieces):
        sig_block, ker_block = pieces
        fft_size = 2 * TOKENS
        product = jnp.fft.rfft(sig_block, n=fft_size, axis=0) * jnp.fft.rfft(ker_block, n=fft_size, axis=0)
        return jnp.fft.irfft(product, n=fft_size, axis=0)[:TOKENS]

    result = lax.map(convolve, (regroup(signal), regroup(kernel)))
    return result.transpose(1, 0, 2).reshape(TOKENS, C).astype(signal.dtype)


def attend(attn_query, attn_keys, attn_values):
    zeros = jnp.zeros((TOK_DEV, KVH * HD), jnp.bfloat16)
    key_pad = jnp.concatenate([zeros, attn_keys], axis=0)
    value_pad = jnp.concatenate([zeros, attn_values], axis=0)
    key_pos = jnp.arange(2 * TOK_DEV, dtype=jnp.int32) - TOK_DEV
    query_pos = jnp.arange(TOK_DEV, dtype=jnp.int32)

    def one_block(block_id):
        start = (block_id * TOK_DEV).astype(jnp.int32)
        queries = lax.dynamic_slice_in_dim(attn_query, start, TOK_DEV, 0).reshape(TOK_DEV, GROUP, KVH, HD)
        key_rows = lax.dynamic_slice_in_dim(key_pad, start, 2 * TOK_DEV, 0).reshape(2 * TOK_DEV, KVH, HD)
        value_rows = lax.dynamic_slice_in_dim(value_pad, start, 2 * TOK_DEV, 0).reshape(2 * TOK_DEV, KVH, HD)
        scores = jnp.einsum("tgjd,sjd->gjts", queries.astype(jnp.float32), key_rows.astype(jnp.float32)) * (HD ** -0.5)
        allowed = (key_pos[None, :] <= query_pos[:, None]) & ((key_pos[None, :] >= 0) | (block_id > 0))
        scores = jnp.where(allowed, scores, jnp.float32(-1e30))
        row_peak = jnp.max(scores, axis=-1)
        expd = jnp.exp(scores - row_peak[..., None])
        row_total = jnp.sum(expd, axis=-1)
        weights = expd.astype(jnp.bfloat16)
        mixed_sum = jnp.einsum("gjts,sjd->tgjd", weights.astype(jnp.float32), value_rows.astype(jnp.float32))
        normed = mixed_sum / row_total.transpose(2, 0, 1)[..., None]
        return normed.astype(jnp.bfloat16).reshape(TOK_DEV, GROUP, KVH * HD), row_peak + jnp.log(row_total)

    outputs, lse_blocks = lax.map(one_block, jnp.arange(N_SEQ, dtype=jnp.int32))
    attn_out = outputs.reshape(TOKENS, GROUP, KVH * HD)
    attn_lse = lse_blocks.transpose(1, 2, 0, 3).reshape(GROUP, KVH, TOKENS)
    return attn_out, attn_lse


def reference(hyena_gate, hyena_key, hyena_value, long_filter, skip_weight, attn_query, attn_keys, attn_values):
    signal = hyena_key.astype(jnp.float32) * hyena_value.astype(jnp.float32)
    kernel = long_filter.astype(jnp.float32)
    conv = long_conv(signal, kernel)
    hyena_out = (hyena_gate.astype(jnp.float32) * (conv + skip_weight * signal)).astype(jnp.bfloat16)
    attn_out, attn_lse = attend(attn_query, attn_keys, attn_values)
    return hyena_out, attn_out, attn_lse
```

```python
import functools
import math

import jax
import jax.numpy as jnp
import numpy as np
from jax import lax
from jax.experimental import pallas as pl
from jax.experimental.pallas import tpu as pltpu
from jax.sharding import PartitionSpec as P

HD = 128
MINOR = 128
ROWS = 256
BIG = -1e30


def hi_lo(x):
    high = x.astype(jnp.bfloat16)
    return high, (x - high.astype(jnp.float32)).astype(jnp.bfloat16)


def split_table(table):
    high = table.astype(jnp.bfloat16)
    low = (table - high.astype(np.float64)).astype(jnp.bfloat16)
    return jnp.asarray(np.stack([high, low]))


def dot3(table_ref, x):
    high, low = hi_lo(x)
    total = jnp.dot(table_ref[0], high, preferred_element_type=jnp.float32)
    total += jnp.dot(table_ref[0], low, preferred_element_type=jnp.float32)
    return total + jnp.dot(table_ref[1], high, preferred_element_type=jnp.float32)


def class_kernel(fwd_ref, inv_ref, twist_ref, sr_ref, si_ref, kr_ref, ki_ref, out_re, out_im):
    for n in range(sr_ref.shape[0]):
        cos = twist_ref[n, :, 0:1]
        sin = twist_ref[n, :, 1:2]

        def spectrum(re, im):
            turned = jnp.concatenate([re * cos + im * sin, im * cos - re * sin], axis=0)
            return dot3(fwd_ref, turned)

        sig = spectrum(sr_ref[n], si_ref[n])
        ker = spectrum(kr_ref[n], ki_ref[n])
        s_re, s_im, k_re, k_im = sig[:MINOR], sig[MINOR:], ker[:MINOR], ker[MINOR:]
        prod = jnp.concatenate([s_re * k_re - s_im * k_im, s_re * k_im + s_im * k_re], axis=0)
        back = dot3(inv_ref, prod)
        b_re, b_im = back[:MINOR], back[MINOR:]
        out_re[n] = b_re * cos - b_im * sin
        out_im[n] = b_im * cos + b_re * sin


def spectra_product(sig, ker, span):
    classes, _, chans = sig[0].shape
    step = max(d for d in range(1, 6) if classes % d == 0)
    index = np.arange(MINOR)
    angle = 2 * math.pi / MINOR * (np.outer(index, index) % MINOR)
    cos, sin = np.cos(angle), np.sin(angle)
    fwd = split_table(np.block([[cos, sin], [-sin, cos]]))
    inv = split_table(np.block([[cos, -sin], [sin, cos]]))
    turn = 2 * math.pi / span * np.outer(np.arange(classes), index)
    twist = jnp.asarray(np.stack([np.cos(turn), np.sin(turn)], axis=-1), jnp.float32)
    table = pl.BlockSpec((2, 2 * MINOR, 2 * MINOR), lambda i: (0, 0, 0))
    block = pl.BlockSpec((step, MINOR, chans), lambda i: (i, 0, 0))
    shape = jax.ShapeDtypeStruct((classes, MINOR, chans), jnp.float32)
    return pl.pallas_call(
        class_kernel,
        grid=(classes // step,),
        in_specs=[table, table, pl.BlockSpec((step, MINOR, 2), lambda i: (i, 0, 0))] + [block] * 4,
        out_specs=[block, block],
        out_shape=[shape, shape],
        compiler_params=pltpu.CompilerParams(vmem_limit_bytes=40 * 1024 * 1024),
        cost_estimate=pl.CostEstimate(
            flops=classes * 18 * 4 * MINOR * MINOR * chans,
            bytes_accessed=classes * MINOR * chans * 24,
            transcendentals=0,
        ),
        name="class_products",
    )(fwd, inv, twist, *sig, *ker)


def line_tables(lines):
    classes = lines // 2 + 1
    angle = 2 * math.pi / lines * (np.outer(np.arange(classes), np.arange(lines // 2)) % lines)
    return np.cos(angle), np.sin(angle)


def spread(blocks):
    cos, sin = line_tables(2 * blocks.shape[0])
    wave = jnp.asarray(np.stack([cos, -sin]), jnp.float32)
    out = jnp.einsum(
        "rpk,kqc->rpqc", wave, blocks.astype(jnp.float32), precision=lax.Precision.HIGH
    )
    return out[0], out[1]


def gather_lines(re, im, lines):
    cos, sin = line_tables(lines)
    weight = np.full((lines // 2 + 1, 1), 2.0)
    weight[0] = weight[-1] = 1.0
    weight /= lines * MINOR
    cos = jnp.asarray((weight * cos).T, jnp.float32)
    sin = jnp.asarray((weight * sin).T, jnp.float32)
    out = jnp.einsum("tp,pqc->tqc", cos, re, precision=lax.Precision.HIGH)
    return out - jnp.einsum("tp,pqc->tqc", sin, im, precision=lax.Precision.HIGH)


def to_channels(x, devices):
    rows, chans = x.shape
    each = chans // devices
    pieces = x.reshape(rows, devices, each).transpose(1, 0, 2)
    got = lax.all_to_all(pieces, "seq", split_axis=0, concat_axis=0, tiled=True)
    return got.reshape(devices * rows // MINOR, MINOR, each)


def to_rows(x, devices):
    lines, _, each = x.shape
    rows = lines * MINOR // devices
    got = lax.all_to_all(
        x.reshape(devices, rows, each), "seq", split_axis=0, concat_axis=0, tiled=True
    )
    return got.transpose(1, 0, 2).reshape(rows, devices * each)


def attend_kernel(groups, bias_ref, q_ref, k_ref, v_ref, out_ref, lse_ref):
    tokens = k_ref.shape[0] // 2
    tile = ROWS // groups
    scale = HD ** (-0.5)
    rate = scale * math.log2(math.e)
    bias = bias_ref[0, 0]
    v_turned = v_ref[...].T
    key_row = lax.broadcasted_iota(jnp.int32, (tile, ROWS), 0)
    query_row = lax.broadcasted_iota(jnp.int32, (tile, ROWS), 1) // groups
    allowed = key_row <= query_row
    for i in range(tokens // tile):
        rows = slice(i * ROWS, (i + 1) * ROWS)
        keys = tokens + (i + 1) * tile
        scores = lax.dot_general(
            k_ref[:keys, :],
            q_ref[rows, :],
            (((1,), (1,)), ((), ())),
            preferred_element_type=jnp.float32,
        )
        pieces = [scores[:tokens] + bias]
        if i:
            pieces.append(scores[tokens : keys - tile])
        pieces.append(jnp.where(allowed, scores[keys - tile :], BIG))
        scores = jnp.concatenate(pieces, axis=0)
        peak = jnp.max(scores, axis=0, keepdims=True)
        weights = jnp.exp2((scores - peak) * rate)
        total = jnp.sum(weights, axis=0, keepdims=True)
        mixed = jnp.dot(
            v_turned[:, :keys],
            weights.astype(jnp.bfloat16),
            preferred_element_type=jnp.float32,
        )
        out_ref[rows, :] = (mixed * (1.0 / total)).T.astype(jnp.bfloat16)
        lse_ref[0, :, rows] = peak * scale + jnp.log(total)


def attend(attn_query, keys, values, my_index):
    tokens, groups, features = attn_query.shape
    heads = features // HD
    rows = tokens * groups
    bias = jnp.where(my_index > 0, 0.0, BIG).astype(jnp.float32).reshape(1, 1)
    column = lambda n: pl.BlockSpec((n, HD), lambda j: (0, j))
    out, lse = pl.pallas_call(
        functools.partial(attend_kernel, groups),
        grid=(heads,),
        in_specs=[
            pl.BlockSpec((1, 1), lambda j: (0, 0), memory_space=pltpu.SMEM),
            column(rows),
            column(2 * tokens),
            column(2 * tokens),
        ],
        out_specs=[column(rows), pl.BlockSpec((1, 1, rows), lambda j: (j, 0, 0))],
        out_shape=[
            jax.ShapeDtypeStruct((rows, features), jnp.bfloat16),
            jax.ShapeDtypeStruct((heads, 1, rows), jnp.float32),
        ],
        compiler_params=pltpu.CompilerParams(vmem_limit_bytes=40 * 1024 * 1024),
        cost_estimate=pl.CostEstimate(
            flops=heads * rows * 2 * tokens * HD * 4,
            bytes_accessed=rows * features * 4 + tokens * features * 8,
            transcendentals=heads * rows * 2 * tokens,
        ),
        name="attend",
    )(bias, attn_query.reshape(rows, features), keys, values)
    lse = lse.reshape(heads, tokens, groups).transpose(2, 0, 1)
    return out.reshape(tokens, groups, features), lse


def local(
    hyena_gate, hyena_key, hyena_value, long_filter, skip_weight, attn_query, attn_keys, attn_values
):
    devices = lax.axis_size("seq")
    my_index = lax.axis_index("seq")
    kv_pair = jnp.stack([attn_keys, attn_values])
    behind = lax.ppermute(kv_pair, "seq", [(i, i + 1) for i in range(devices - 1)])
    ker_blocks = to_channels(long_filter, devices)
    signal = hyena_key.astype(jnp.float32) * hyena_value.astype(jnp.float32)
    sig_blocks = to_channels(signal.astype(jnp.bfloat16), devices)
    window = jnp.concatenate([behind, kv_pair], axis=1)
    window = lax.all_gather(window, "chan", axis=2, tiled=True)
    attn_out, attn_lse = attend(attn_query, window[0], window[1], my_index)
    lines = 2 * ker_blocks.shape[0]
    ker = spread(ker_blocks)
    sig = spread(sig_blocks)
    back = spectra_product(sig, ker, lines * MINOR)
    conv = to_rows(gather_lines(*back, lines).astype(jnp.bfloat16), devices)
    signal = hyena_key.astype(jnp.float32) * hyena_value.astype(jnp.float32)
    hyena_out = hyena_gate.astype(jnp.float32) * (
        conv.astype(jnp.float32) + skip_weight * signal
    )
    return (hyena_out.astype(jnp.bfloat16), attn_out, attn_lse)


def solution(mesh):
    return jax.shard_map(
        local,
        mesh=mesh,
        in_specs=(
            P("seq", "chan"),
            P("seq", "chan"),
            P("seq", "chan"),
            P("seq", "chan"),
            P("chan"),
            P("seq", "chan", None),
            P("seq", "chan"),
            P("seq", "chan"),
        ),
        out_specs=(P("seq", "chan"), P("seq", "chan", None), P("chan", None, "seq")),
        check_vma=False,
    )
```

```python
import functools
import math

import jax
import jax.numpy as jnp
import numpy as np
from jax import lax
from jax.experimental import pallas as pl
from jax.experimental.pallas import tpu as pltpu
from jax.sharding import PartitionSpec as P

HD = 128
MINOR = 128
ROWS = 256
BIG = -1e30


def hi_lo(x):
    high = x.astype(jnp.bfloat16)
    return high, (x - high.astype(jnp.float32)).astype(jnp.bfloat16)


def split_table(table):
    high = table.astype(jnp.bfloat16)
    low = (table - high.astype(np.float64)).astype(jnp.bfloat16)
    return jnp.asarray(np.stack([high, low]))


def dot3(table_ref, x):
    high, low = hi_lo(x)
    total = jnp.dot(table_ref[0], high, preferred_element_type=jnp.float32)
    total += jnp.dot(table_ref[0], low, preferred_element_type=jnp.float32)
    return total + jnp.dot(table_ref[1], high, preferred_element_type=jnp.float32)


def class_kernel(fwd_ref, inv_ref, twist_ref, sr_ref, si_ref, kr_ref, ki_ref, out_re, out_im):
    for n in range(sr_ref.shape[0]):
        cos = twist_ref[n, :, 0:1]
        sin = twist_ref[n, :, 1:2]

        def spectrum(re, im):
            turned = jnp.concatenate([re * cos + im * sin, im * cos - re * sin], axis=0)
            return dot3(fwd_ref, turned)

        sig = spectrum(sr_ref[n], si_ref[n])
        ker = spectrum(kr_ref[n], ki_ref[n])
        s_re, s_im, k_re, k_im = sig[:MINOR], sig[MINOR:], ker[:MINOR], ker[MINOR:]
        prod = jnp.concatenate([s_re * k_re - s_im * k_im, s_re * k_im + s_im * k_re], axis=0)
        back = dot3(inv_ref, prod)
        b_re, b_im = back[:MINOR], back[MINOR:]
        out_re[n] = b_re * cos - b_im * sin
        out_im[n] = b_im * cos + b_re * sin


def spectra_product(sig, ker, span):
    classes, _, chans = sig[0].shape
    step = max(d for d in range(1, 6) if classes % d == 0)
    index = np.arange(MINOR)
    angle = 2 * math.pi / MINOR * (np.outer(index, index) % MINOR)
    cos, sin = np.cos(angle), np.sin(angle)
    fwd = split_table(np.block([[cos, sin], [-sin, cos]]))
    inv = split_table(np.block([[cos, -sin], [sin, cos]]))
    turn = 2 * math.pi / span * np.outer(np.arange(classes), index)
    twist = jnp.asarray(np.stack([np.cos(turn), np.sin(turn)], axis=-1), jnp.float32)
    table = pl.BlockSpec((2, 2 * MINOR, 2 * MINOR), lambda i: (0, 0, 0))
    block = pl.BlockSpec((step, MINOR, chans), lambda i: (i, 0, 0))
    shape = jax.ShapeDtypeStruct((classes, MINOR, chans), jnp.float32)
    return pl.pallas_call(
        class_kernel,
        grid=(classes // step,),
        in_specs=[table, table, pl.BlockSpec((step, MINOR, 2), lambda i: (i, 0, 0))] + [block] * 4,
        out_specs=[block, block],
        out_shape=[shape, shape],
        compiler_params=pltpu.CompilerParams(vmem_limit_bytes=40 * 1024 * 1024),
        cost_estimate=pl.CostEstimate(
            flops=classes * 18 * 4 * MINOR * MINOR * chans,
            bytes_accessed=classes * MINOR * chans * 24,
            transcendentals=0,
        ),
        name="class_products",
    )(fwd, inv, twist, *sig, *ker)


def line_tables(lines):
    classes = lines // 2 + 1
    angle = 2 * math.pi / lines * (np.outer(np.arange(classes), np.arange(lines // 2)) % lines)
    return np.cos(angle), np.sin(angle)


def spread(blocks):
    cos, sin = line_tables(2 * blocks.shape[0])
    wave = jnp.asarray(np.stack([cos, -sin]), jnp.float32)
    out = jnp.einsum(
        "rpk,kqc->rpqc", wave, blocks.astype(jnp.float32), precision=lax.Precision.HIGH
    )
    return out[0], out[1]


def gather_lines(re, im, lines):
    cos, sin = line_tables(lines)
    weight = np.full((lines // 2 + 1, 1), 2.0)
    weight[0] = weight[-1] = 1.0
    weight /= lines * MINOR
    cos = jnp.asarray((weight * cos).T, jnp.float32)
    sin = jnp.asarray((weight * sin).T, jnp.float32)
    out = jnp.einsum("tp,pqc->tqc", cos, re, precision=lax.Precision.HIGH)
    return out - jnp.einsum("tp,pqc->tqc", sin, im, precision=lax.Precision.HIGH)


def attend_kernel(groups, bias_ref, q_ref, kp_ref, vp_ref, ko_ref, vo_ref, out_ref, lse_ref):
    tokens = ko_ref.shape[1]
    tile = ROWS // groups
    scale = HD ** (-0.5)
    rate = scale * math.log2(math.e)
    bias = bias_ref[0, 0]
    v_before = vp_ref[0].T
    v_own = vo_ref[0].T
    key_row = lax.broadcasted_iota(jnp.int32, (tile, ROWS), 0)
    query_row = lax.broadcasted_iota(jnp.int32, (tile, ROWS), 1) // groups
    allowed = key_row <= query_row
    contract = functools.partial(
        lax.dot_general,
        dimension_numbers=(((1,), (1,)), ((), ())),
        preferred_element_type=jnp.float32,
    )
    for i in range(tokens // tile):
        rows = slice(i * ROWS, (i + 1) * ROWS)
        keys = (i + 1) * tile
        query = q_ref[rows, :]
        before = contract(kp_ref[0], query) + bias
        own = contract(ko_ref[0, :keys, :], query)
        last = jnp.where(allowed, own[keys - tile :], BIG)
        own = jnp.concatenate([own[: keys - tile], last], axis=0) if i else last
        peak = jnp.maximum(
            jnp.max(before, axis=0, keepdims=True), jnp.max(own, axis=0, keepdims=True)
        )
        before = jnp.exp2((before - peak) * rate)
        own = jnp.exp2((own - peak) * rate)
        total = jnp.sum(before, axis=0, keepdims=True) + jnp.sum(own, axis=0, keepdims=True)
        mixed = jnp.dot(
            v_before, before.astype(jnp.bfloat16), preferred_element_type=jnp.float32
        ) + jnp.dot(v_own[:, :keys], own.astype(jnp.bfloat16), preferred_element_type=jnp.float32)
        out_ref[rows, :] = (mixed * (1.0 / total)).T.astype(jnp.bfloat16)
        lse_ref[0, :, rows] = peak * scale + jnp.log(total)


def attend(queries, groups, behind, own, my_index):
    rows, features = queries.shape
    tokens = rows // groups
    heads = features // HD
    bias = jnp.where(my_index > 0, 0.0, BIG).astype(jnp.float32).reshape(1, 1)
    column = pl.BlockSpec((rows, HD), lambda j: (0, j))
    keys = pl.BlockSpec((1, tokens, HD), lambda j: (0, 0, j))
    values = pl.BlockSpec((1, tokens, HD), lambda j: (1, 0, j))
    return pl.pallas_call(
        functools.partial(attend_kernel, groups),
        grid=(heads,),
        in_specs=[
            pl.BlockSpec((1, 1), lambda j: (0, 0), memory_space=pltpu.SMEM),
            column,
            keys,
            values,
            keys,
            values,
        ],
        out_specs=[column, pl.BlockSpec((1, 1, rows), lambda j: (j, 0, 0))],
        out_shape=[
            jax.ShapeDtypeStruct((rows, features), jnp.bfloat16),
            jax.ShapeDtypeStruct((heads, 1, rows), jnp.float32),
        ],
        compiler_params=pltpu.CompilerParams(vmem_limit_bytes=40 * 1024 * 1024),
        cost_estimate=pl.CostEstimate(
            flops=heads * rows * 2 * tokens * HD * 4,
            bytes_accessed=rows * features * 4 + tokens * features * 8,
            transcendentals=heads * rows * 2 * tokens,
        ),
        name="attend",
    )(bias, queries, behind, behind, own, own)


def conv_kernel(w1_ref, w2_ref, fwd_ref, inv_ref, twist_ref, sig_ref, ker_ref, out_ref,
                wide_ref, sig_lines, ker_lines):
    half = sig_ref.shape[0] // MINOR
    both = w1_ref.shape[0]
    slots = both // 2
    chans = sig_ref.shape[1]
    piece = min(1024, sig_ref.shape[0])

    for source, lines in ((sig_ref, sig_lines), (ker_ref, ker_lines)):

        def widen(i, _):
            at = pl.ds(pl.multiple_of(i * piece, piece), piece)
            wide_ref[at, :] = source[at, :].astype(jnp.float32)
            return 0

        lax.fori_loop(0, source.shape[0] // piece, widen, 0)

        def first(i, _):
            cols = [wide_ref[pl.ds(2 * i + d, half, stride=MINOR), :] for d in range(2)]
            col = jnp.concatenate(cols, axis=1).astype(jnp.bfloat16)
            got = jnp.dot(
                w1_ref[...],
                jnp.concatenate([col, col], axis=0),
                preferred_element_type=jnp.float32,
            )
            for d in range(2):
                at = pl.ds(pl.multiple_of((2 * i + d) * both, 8), both)
                lines[at, :] = got[:, d * chans : (d + 1) * chans]
            return 0

        lax.fori_loop(0, MINOR // 2, first, 0, unroll=2)

    def pair(i, _):
        prods, turns = [], []
        for d in range(2):
            n = 2 * i + d
            at_re = pl.ds(n, MINOR, stride=both)
            at_im = pl.ds(n + slots, MINOR, stride=both)
            turn = twist_ref[n]
            cos, sin = turn[:, 0:1], turn[:, 1:2]
            re = jnp.concatenate([sig_lines[at_re, :], ker_lines[at_re, :]], axis=1)
            im = jnp.concatenate([sig_lines[at_im, :], ker_lines[at_im, :]], axis=1)
            turned = jnp.concatenate([re * cos + im * sin, im * cos - re * sin], axis=0)
            spec = dot3(fwd_ref, turned)
            s_re, k_re = spec[:MINOR, :chans], spec[:MINOR, chans:]
            s_im, k_im = spec[MINOR:, :chans], spec[MINOR:, chans:]
            prods.append(
                jnp.concatenate([s_re * k_re - s_im * k_im, s_re * k_im + s_im * k_re], axis=0)
            )
            turns.append((at_re, at_im, cos, sin))
        back = dot3(inv_ref, jnp.concatenate(prods, axis=1))
        for d, (at_re, at_im, cos, sin) in enumerate(turns):
            b_re = back[:MINOR, d * chans : (d + 1) * chans]
            b_im = back[MINOR:, d * chans : (d + 1) * chans]
            sig_lines[at_re, :] = b_re * cos - b_im * sin
            sig_lines[at_im, :] = b_im * cos + b_re * sin
        return 0

    lax.fori_loop(0, twist_ref.shape[0] // 2, pair, 0)

    def last(i, _):
        cols = [
            sig_lines[pl.ds(pl.multiple_of((2 * i + d) * both, 8), both), :] for d in range(2)
        ]
        high, low = hi_lo(jnp.concatenate(cols, axis=1))
        got = jnp.dot(
            w2_ref[...],
            jnp.concatenate([high, low, high], axis=0),
            preferred_element_type=jnp.float32,
        )
        for d in range(2):
            wide_ref[pl.ds(2 * i + d, half, stride=MINOR), :] = got[:, d * chans : (d + 1) * chans]
        return 0

    lax.fori_loop(0, MINOR // 2, last, 0, unroll=2)

    def narrow(i, _):
        at = pl.ds(pl.multiple_of(i * piece, piece), piece)
        out_ref[at, :] = wide_ref[at, :].astype(jnp.bfloat16)
        return 0

    lax.fori_loop(0, out_ref.shape[0] // piece, narrow, 0)


def whole_conv(sig, ker):
    length, chans = sig.shape
    half = length // MINOR
    lines, span = 2 * half, 2 * length
    classes = half + 1
    slots = -(-classes // 16) * 16
    cos, sin = line_tables(lines)
    w1 = np.zeros((2, slots, half))
    w1[0, :classes], w1[1, :classes] = cos, -sin
    w1 = split_table(w1.reshape(2 * slots, half))
    weight = np.full((classes, 1), 2.0)
    weight[0] = weight[-1] = 1.0
    weight /= span
    w2 = np.zeros((2, slots, half))
    w2[0, :classes], w2[1, :classes] = weight * cos, -weight * sin
    w2 = split_table(w2.reshape(2 * slots, half).T)
    w1 = jnp.concatenate([w1[0], w1[1]], axis=1)
    w2 = jnp.concatenate([w2[0], w2[0], w2[1]], axis=1)
    index = np.arange(MINOR)
    angle = 2 * math.pi / MINOR * (np.outer(index, index) % MINOR)
    cos, sin = np.cos(angle), np.sin(angle)
    fwd = split_table(np.block([[cos, sin], [-sin, cos]]))
    inv = split_table(np.block([[cos, -sin], [sin, cos]]))
    turn = 2 * math.pi / span * np.outer(np.arange(classes + classes % 2), index)
    twist = jnp.asarray(np.stack([np.cos(turn), np.sin(turn)], axis=-1), jnp.float32)
    vmem = pl.BlockSpec(memory_space=pltpu.VMEM)
    return pl.pallas_call(
        conv_kernel,
        in_specs=[vmem] * 7,
        out_specs=vmem,
        out_shape=jax.ShapeDtypeStruct((length, chans), jnp.bfloat16),
        scratch_shapes=[
            pltpu.VMEM((length, chans), jnp.float32),
            pltpu.VMEM((MINOR * 2 * slots, chans), jnp.float32),
            pltpu.VMEM((MINOR * 2 * slots, chans), jnp.float32),
        ],
        compiler_params=pltpu.CompilerParams(vmem_limit_bytes=48 * 1024 * 1024),
        cost_estimate=pl.CostEstimate(
            flops=classes * 18 * 4 * MINOR * MINOR * chans,
            bytes_accessed=length * chans * 6,
            transcendentals=0,
        ),
        name="whole_conv",
    )(w1, w2, fwd, inv, twist, sig, ker)


def prepare_kernel(key_ref, value_ref, filter_ref, sig_ref, ker_ref):
    each = sig_ref.shape[2]
    for n in range(sig_ref.shape[0]):
        at = slice(n * each, (n + 1) * each)
        signal = key_ref[:, at].astype(jnp.float32) * value_ref[:, at].astype(jnp.float32)
        sig_ref[n] = signal.astype(jnp.bfloat16)
        ker_ref[n] = filter_ref[:, at]


def finish_kernel(gate_ref, key_ref, value_ref, skip_ref, conv_ref, out_ref):
    each = conv_ref.shape[2]
    for n in range(conv_ref.shape[0]):
        at = slice(n * each, (n + 1) * each)
        signal = key_ref[:, at].astype(jnp.float32) * value_ref[:, at].astype(jnp.float32)
        out = gate_ref[:, at].astype(jnp.float32) * (
            conv_ref[n].astype(jnp.float32) + skip_ref[:, at] * signal
        )
        out_ref[:, at] = out.astype(jnp.bfloat16)


def by_groups(kernel, flat, rowed, pieces, outs, devices, name):
    rows, chans = flat[0].shape
    each = chans // devices
    step = 4 if devices % 4 == 0 else 1
    whole = pl.BlockSpec((rows, step * each), lambda i: (0, i))
    thin = pl.BlockSpec((1, step * each), lambda i: (0, i))
    split = pl.BlockSpec((step, rows, each), lambda i: (i, 0, 0))
    shape = (devices, rows, each) if outs == 2 else (rows, chans)
    return pl.pallas_call(
        kernel,
        grid=(devices // step,),
        in_specs=[whole] * len(flat) + [thin] * len(rowed) + [split] * len(pieces),
        out_specs=[split, split] if outs == 2 else whole,
        out_shape=[jax.ShapeDtypeStruct(shape, jnp.bfloat16)] * 2
        if outs == 2
        else jax.ShapeDtypeStruct(shape, jnp.bfloat16),
        compiler_params=pltpu.CompilerParams(vmem_limit_bytes=40 * 1024 * 1024),
        cost_estimate=pl.CostEstimate(
            flops=rows * chans * 4, bytes_accessed=rows * chans * 10, transcendentals=0
        ),
        name=name,
    )(*flat, *rowed, *pieces)


def exchange(x):
    return lax.all_to_all(x, "seq", split_axis=0, concat_axis=0, tiled=True)


def local(
    hyena_gate, hyena_key, hyena_value, long_filter, skip_weight, attn_query, attn_keys, attn_values
):
    devices = lax.axis_size("seq")
    my_index = lax.axis_index("seq")
    rows, chans = hyena_key.shape
    each = chans // devices
    aligned = each % 128 == 0
    kv_pair = jnp.stack([attn_keys, attn_values])
    behind = lax.ppermute(kv_pair, "seq", [(i, i + 1) for i in range(devices - 1)])
    own = lax.all_gather(kv_pair, "chan", axis=2, tiled=True)
    if aligned:
        sig, ker = by_groups(
            prepare_kernel, (hyena_key, hyena_value, long_filter), (), (), 2, devices, "prepare"
        )
    else:
        signal = hyena_key.astype(jnp.float32) * hyena_value.astype(jnp.float32)
        sig, ker = (
            x.reshape(rows, devices, each).transpose(1, 0, 2)
            for x in (signal.astype(jnp.bfloat16), long_filter)
        )
    behind, sig, ker = lax.optimization_barrier((behind, sig, ker))
    ker, sig = exchange(ker), exchange(sig)
    behind = lax.all_gather(behind, "chan", axis=2, tiled=True)
    tokens, groups, features = attn_query.shape
    queries = attn_query.reshape(tokens * groups, features)
    out, lse = attend(queries, groups, behind, own, my_index)
    out, lse, sig, ker = lax.optimization_barrier((out, lse, sig, ker))
    if aligned:
        flat = (devices * rows, each)
        conv = whole_conv(sig.reshape(flat), ker.reshape(flat)).reshape(sig.shape)
        hyena_out = by_groups(
            finish_kernel,
            (hyena_gate, hyena_key, hyena_value),
            (skip_weight[None, :],),
            (exchange(conv),),
            1,
            devices,
            "finish",
        )
    else:
        cube = (devices * rows // MINOR, MINOR, each)
        lines = 2 * cube[0]
        back = spectra_product(spread(sig.reshape(cube)), spread(ker.reshape(cube)), lines * MINOR)
        conv = gather_lines(*back, lines).astype(jnp.bfloat16)
        conv = exchange(conv.reshape(sig.shape)).transpose(1, 0, 2).reshape(rows, chans)
        signal = hyena_key.astype(jnp.float32) * hyena_value.astype(jnp.float32)
        hyena_out = hyena_gate.astype(jnp.float32) * (
            conv.astype(jnp.float32) + skip_weight * signal
        )
        hyena_out = hyena_out.astype(jnp.bfloat16)
    attn_lse = lse.reshape(features // HD, tokens, groups).transpose(2, 0, 1)
    return (hyena_out, out.reshape(attn_query.shape), attn_lse)


def solution(mesh):
    return jax.shard_map(
        local,
        mesh=mesh,
        in_specs=(
            P("seq", "chan"),
            P("seq", "chan"),
            P("seq", "chan"),
            P("seq", "chan"),
            P("chan"),
            P("seq", "chan", None),
            P("seq", "chan"),
            P("seq", "chan"),
        ),
        out_specs=(P("seq", "chan"), P("seq", "chan", None), P("chan", None, "seq")),
        check_vma=False,
    )
```

```python
import functools
import math

import jax
import jax.numpy as jnp
import numpy as np
from jax import lax
from jax.experimental import pallas as pl
from jax.experimental.pallas import tpu as pltpu
from jax.sharding import PartitionSpec as P

HD = 128
MINOR = 128
ROWS = 256
BIG = -1e30


def hi_lo(x):
    high = x.astype(jnp.bfloat16)
    return high, (x - high.astype(jnp.float32)).astype(jnp.bfloat16)


def split_table(table):
    high = table.astype(jnp.bfloat16)
    low = (table - high.astype(np.float64)).astype(jnp.bfloat16)
    return jnp.asarray(np.stack([high, low]))


def dot3(table_ref, x):
    high, low = hi_lo(x)
    total = jnp.dot(table_ref[0], high, preferred_element_type=jnp.float32)
    total += jnp.dot(table_ref[0], low, preferred_element_type=jnp.float32)
    return total + jnp.dot(table_ref[1], high, preferred_element_type=jnp.float32)


def class_kernel(fwd_ref, inv_ref, twist_ref, sr_ref, si_ref, kr_ref, ki_ref, out_re, out_im):
    for n in range(sr_ref.shape[0]):
        cos = twist_ref[n, :, 0:1]
        sin = twist_ref[n, :, 1:2]

        def spectrum(re, im):
            turned = jnp.concatenate([re * cos + im * sin, im * cos - re * sin], axis=0)
            return dot3(fwd_ref, turned)

        sig = spectrum(sr_ref[n], si_ref[n])
        ker = spectrum(kr_ref[n], ki_ref[n])
        s_re, s_im, k_re, k_im = sig[:MINOR], sig[MINOR:], ker[:MINOR], ker[MINOR:]
        prod = jnp.concatenate([s_re * k_re - s_im * k_im, s_re * k_im + s_im * k_re], axis=0)
        back = dot3(inv_ref, prod)
        b_re, b_im = back[:MINOR], back[MINOR:]
        out_re[n] = b_re * cos - b_im * sin
        out_im[n] = b_im * cos + b_re * sin


def spectra_product(sig, ker, span):
    classes, _, chans = sig[0].shape
    step = max(d for d in range(1, 6) if classes % d == 0)
    index = np.arange(MINOR)
    angle = 2 * math.pi / MINOR * (np.outer(index, index) % MINOR)
    cos, sin = np.cos(angle), np.sin(angle)
    fwd = split_table(np.block([[cos, sin], [-sin, cos]]))
    inv = split_table(np.block([[cos, -sin], [sin, cos]]))
    turn = 2 * math.pi / span * np.outer(np.arange(classes), index)
    twist = jnp.asarray(np.stack([np.cos(turn), np.sin(turn)], axis=-1), jnp.float32)
    table = pl.BlockSpec((2, 2 * MINOR, 2 * MINOR), lambda i: (0, 0, 0))
    block = pl.BlockSpec((step, MINOR, chans), lambda i: (i, 0, 0))
    shape = jax.ShapeDtypeStruct((classes, MINOR, chans), jnp.float32)
    return pl.pallas_call(
        class_kernel,
        grid=(classes // step,),
        in_specs=[table, table, pl.BlockSpec((step, MINOR, 2), lambda i: (i, 0, 0))] + [block] * 4,
        out_specs=[block, block],
        out_shape=[shape, shape],
        compiler_params=pltpu.CompilerParams(vmem_limit_bytes=40 * 1024 * 1024),
        cost_estimate=pl.CostEstimate(
            flops=classes * 18 * 4 * MINOR * MINOR * chans,
            bytes_accessed=classes * MINOR * chans * 24,
            transcendentals=0,
        ),
        name="class_products",
    )(fwd, inv, twist, *sig, *ker)


def line_tables(lines):
    classes = lines // 2 + 1
    angle = 2 * math.pi / lines * (np.outer(np.arange(classes), np.arange(lines // 2)) % lines)
    return np.cos(angle), np.sin(angle)


def spread(blocks):
    cos, sin = line_tables(2 * blocks.shape[0])
    wave = jnp.asarray(np.stack([cos, -sin]), jnp.float32)
    out = jnp.einsum(
        "rpk,kqc->rpqc", wave, blocks.astype(jnp.float32), precision=lax.Precision.HIGH
    )
    return out[0], out[1]


def gather_lines(re, im, lines):
    cos, sin = line_tables(lines)
    weight = np.full((lines // 2 + 1, 1), 2.0)
    weight[0] = weight[-1] = 1.0
    weight /= lines * MINOR
    cos = jnp.asarray((weight * cos).T, jnp.float32)
    sin = jnp.asarray((weight * sin).T, jnp.float32)
    out = jnp.einsum("tp,pqc->tqc", cos, re, precision=lax.Precision.HIGH)
    return out - jnp.einsum("tp,pqc->tqc", sin, im, precision=lax.Precision.HIGH)


def attend_kernel(groups, bias_ref, q_ref, kp_ref, vp_ref, ko_ref, vo_ref, out_ref, lse_ref):
    tokens = ko_ref.shape[1]
    tile = ROWS // groups
    scale = HD ** (-0.5)
    rate = scale * math.log2(math.e)
    bias = bias_ref[0, 0]
    v_before = vp_ref[0].T
    v_own = vo_ref[0].T
    key_row = lax.broadcasted_iota(jnp.int32, (tile, ROWS), 0)
    query_row = lax.broadcasted_iota(jnp.int32, (tile, ROWS), 1) // groups
    allowed = key_row <= query_row
    contract = functools.partial(
        lax.dot_general,
        dimension_numbers=(((1,), (1,)), ((), ())),
        preferred_element_type=jnp.float32,
    )
    for i in range(tokens // tile):
        rows = slice(i * ROWS, (i + 1) * ROWS)
        keys = (i + 1) * tile
        query = q_ref[rows, :]
        before = contract(kp_ref[0], query) + bias
        own = contract(ko_ref[0, :keys, :], query)
        last = jnp.where(allowed, own[keys - tile :], BIG)
        own = jnp.concatenate([own[: keys - tile], last], axis=0) if i else last
        peak = jnp.maximum(
            jnp.max(before, axis=0, keepdims=True), jnp.max(own, axis=0, keepdims=True)
        )
        before = jnp.exp2((before - peak) * rate)
        own = jnp.exp2((own - peak) * rate)
        total = jnp.sum(before, axis=0, keepdims=True) + jnp.sum(own, axis=0, keepdims=True)
        mixed = jnp.dot(
            v_before, before.astype(jnp.bfloat16), preferred_element_type=jnp.float32
        ) + jnp.dot(v_own[:, :keys], own.astype(jnp.bfloat16), preferred_element_type=jnp.float32)
        out_ref[rows, :] = (mixed * (1.0 / total)).T.astype(jnp.bfloat16)
        lse_ref[0, :, rows] = peak * scale + jnp.log(total)


def attend(queries, groups, behind, own, my_index):
    rows, features = queries.shape
    tokens = rows // groups
    heads = features // HD
    bias = jnp.where(my_index > 0, 0.0, BIG).astype(jnp.float32).reshape(1, 1)
    column = pl.BlockSpec((rows, HD), lambda j: (0, j))
    keys = pl.BlockSpec((1, tokens, HD), lambda j: (0, 0, j))
    values = pl.BlockSpec((1, tokens, HD), lambda j: (1, 0, j))
    return pl.pallas_call(
        functools.partial(attend_kernel, groups),
        grid=(heads,),
        in_specs=[
            pl.BlockSpec((1, 1), lambda j: (0, 0), memory_space=pltpu.SMEM),
            column,
            keys,
            values,
            keys,
            values,
        ],
        out_specs=[column, pl.BlockSpec((1, 1, rows), lambda j: (j, 0, 0))],
        out_shape=[
            jax.ShapeDtypeStruct((rows, features), jnp.bfloat16),
            jax.ShapeDtypeStruct((heads, 1, rows), jnp.float32),
        ],
        compiler_params=pltpu.CompilerParams(vmem_limit_bytes=40 * 1024 * 1024),
        cost_estimate=pl.CostEstimate(
            flops=heads * rows * 2 * tokens * HD * 4,
            bytes_accessed=rows * features * 4 + tokens * features * 8,
            transcendentals=heads * rows * 2 * tokens,
        ),
        name="attend",
    )(bias, queries, behind, behind, own, own)


def conv_kernel(w1_ref, w2_ref, fwd_ref, inv_ref, twist_ref, both_ref, out_ref,
                wide_ref, sig_lines, ker_lines):
    devices, rows = both_ref.shape[0], both_ref.shape[1] // 2
    half = wide_ref.shape[0] // MINOR
    both = w1_ref.shape[0]
    slots = both // 2
    chans = wide_ref.shape[1]

    for offset, lines in ((0, sig_lines), (rows, ker_lines)):

        def widen(i, _):
            at = pl.ds(pl.multiple_of(i * rows, rows), rows)
            wide_ref[at, :] = both_ref[i, offset : offset + rows, :].astype(jnp.float32)
            return 0

        lax.fori_loop(0, devices, widen, 0)

        def first(i, _):
            cols = [wide_ref[pl.ds(2 * i + d, half, stride=MINOR), :] for d in range(2)]
            col = jnp.concatenate(cols, axis=1).astype(jnp.bfloat16)
            got = jnp.dot(
                w1_ref[...],
                jnp.concatenate([col, col], axis=0),
                preferred_element_type=jnp.float32,
            )
            for d in range(2):
                at = pl.ds(pl.multiple_of((2 * i + d) * both, 8), both)
                lines[at, :] = got[:, d * chans : (d + 1) * chans]
            return 0

        lax.fori_loop(0, MINOR // 2, first, 0, unroll=4)

    def several(i, _):
        loaded = []
        for d in range(4):
            n = 4 * i + d
            at_re = pl.ds(n, MINOR, stride=both)
            at_im = pl.ds(n + slots, MINOR, stride=both)
            turn = twist_ref[n]
            re = jnp.concatenate([sig_lines[at_re, :], ker_lines[at_re, :]], axis=1)
            im = jnp.concatenate([sig_lines[at_im, :], ker_lines[at_im, :]], axis=1)
            loaded.append((at_re, at_im, turn[:, 0:1], turn[:, 1:2], re, im))
        prods = []
        for _, _, cos, sin, re, im in loaded:
            turned = jnp.concatenate([re * cos + im * sin, im * cos - re * sin], axis=0)
            spec = dot3(fwd_ref, turned)
            s_re, k_re = spec[:MINOR, :chans], spec[:MINOR, chans:]
            s_im, k_im = spec[MINOR:, :chans], spec[MINOR:, chans:]
            prods.append(
                jnp.concatenate([s_re * k_re - s_im * k_im, s_re * k_im + s_im * k_re], axis=0)
            )
        backs = [dot3(inv_ref, jnp.concatenate(prods[d : d + 2], axis=1)) for d in (0, 2)]
        for d, (at_re, at_im, cos, sin, _, _) in enumerate(loaded):
            back = backs[d // 2][:, (d % 2) * chans : (d % 2 + 1) * chans]
            b_re, b_im = back[:MINOR], back[MINOR:]
            sig_lines[at_re, :] = b_re * cos - b_im * sin
            sig_lines[at_im, :] = b_im * cos + b_re * sin
        return 0

    lax.fori_loop(0, twist_ref.shape[0] // 4, several, 0)

    def last(i, _):
        cols = [
            sig_lines[pl.ds(pl.multiple_of((2 * i + d) * both, 8), both), :] for d in range(2)
        ]
        high, low = hi_lo(jnp.concatenate(cols, axis=1))
        got = jnp.dot(
            w2_ref[...],
            jnp.concatenate([high, low, high], axis=0),
            preferred_element_type=jnp.float32,
        )
        for d in range(2):
            wide_ref[pl.ds(2 * i + d, half, stride=MINOR), :] = got[:, d * chans : (d + 1) * chans]
        return 0

    lax.fori_loop(0, MINOR // 2, last, 0, unroll=4)

    def narrow(i, _):
        at = pl.ds(pl.multiple_of(i * rows, rows), rows)
        out_ref[i] = wide_ref[at, :].astype(jnp.bfloat16)
        return 0

    lax.fori_loop(0, devices, narrow, 0)


def whole_conv(both):
    devices, rows, chans = both.shape
    rows = rows // 2
    length = devices * rows
    half = length // MINOR
    lines, span = 2 * half, 2 * length
    classes = half + 1
    slots = -(-classes // 8) * 8
    cos, sin = line_tables(lines)
    w1 = np.zeros((2, slots, half))
    w1[0, :classes], w1[1, :classes] = cos, -sin
    w1 = split_table(w1.reshape(2 * slots, half))
    weight = np.full((classes, 1), 2.0)
    weight[0] = weight[-1] = 1.0
    weight /= span
    w2 = np.zeros((2, slots, half))
    w2[0, :classes], w2[1, :classes] = weight * cos, -weight * sin
    w2 = split_table(w2.reshape(2 * slots, half).T)
    w1 = jnp.concatenate([w1[0], w1[1]], axis=1)
    w2 = jnp.concatenate([w2[0], w2[0], w2[1]], axis=1)
    index = np.arange(MINOR)
    angle = 2 * math.pi / MINOR * (np.outer(index, index) % MINOR)
    cos, sin = np.cos(angle), np.sin(angle)
    fwd = split_table(np.block([[cos, sin], [-sin, cos]]))
    inv = split_table(np.block([[cos, -sin], [sin, cos]]))
    turn = 2 * math.pi / span * np.outer(np.arange(-(-classes // 4) * 4), index)
    twist = jnp.asarray(np.stack([np.cos(turn), np.sin(turn)], axis=-1), jnp.float32)
    vmem = pl.BlockSpec(memory_space=pltpu.VMEM)
    return pl.pallas_call(
        conv_kernel,
        in_specs=[vmem] * 6,
        out_specs=vmem,
        out_shape=jax.ShapeDtypeStruct((devices, rows, chans), jnp.bfloat16),
        scratch_shapes=[
            pltpu.VMEM((length, chans), jnp.float32),
            pltpu.VMEM((MINOR * 2 * slots, chans), jnp.float32),
            pltpu.VMEM((MINOR * 2 * slots, chans), jnp.float32),
        ],
        compiler_params=pltpu.CompilerParams(vmem_limit_bytes=48 * 1024 * 1024),
        cost_estimate=pl.CostEstimate(
            flops=classes * 18 * 4 * MINOR * MINOR * chans,
            bytes_accessed=length * chans * 6,
            transcendentals=0,
        ),
        name="whole_conv",
    )(w1, w2, fwd, inv, twist, both)


def prepare_kernel(key_ref, value_ref, filter_ref, both_ref):
    rows, each = key_ref.shape[0], both_ref.shape[2]
    for n in range(both_ref.shape[0]):
        at = slice(n * each, (n + 1) * each)
        signal = key_ref[:, at].astype(jnp.float32) * value_ref[:, at].astype(jnp.float32)
        both_ref[n, :rows] = signal.astype(jnp.bfloat16)
        both_ref[n, rows:] = filter_ref[:, at]


def finish_kernel(gate_ref, key_ref, value_ref, skip_ref, conv_ref, out_ref):
    each = conv_ref.shape[2]
    for n in range(conv_ref.shape[0]):
        at = slice(n * each, (n + 1) * each)
        signal = key_ref[:, at].astype(jnp.float32) * value_ref[:, at].astype(jnp.float32)
        out = gate_ref[:, at].astype(jnp.float32) * (
            conv_ref[n].astype(jnp.float32) + skip_ref[:, at] * signal
        )
        out_ref[:, at] = out.astype(jnp.bfloat16)


def by_groups(kernel, flat, rowed, pieces, shape, devices, name):
    rows, chans = flat[0].shape
    each = chans // devices
    step = 4 if devices % 4 == 0 else 1
    whole = pl.BlockSpec((rows, step * each), lambda i: (0, i))
    thin = pl.BlockSpec((1, step * each), lambda i: (0, i))
    split = pl.BlockSpec((step, rows, each), lambda i: (i, 0, 0))
    widened = pl.BlockSpec((step, 2 * rows, each), lambda i: (i, 0, 0))
    return pl.pallas_call(
        kernel,
        grid=(devices // step,),
        in_specs=[whole] * len(flat) + [thin] * len(rowed) + [split] * len(pieces),
        out_specs=whole if len(shape) == 2 else widened,
        out_shape=jax.ShapeDtypeStruct(shape, jnp.bfloat16),
        compiler_params=pltpu.CompilerParams(vmem_limit_bytes=40 * 1024 * 1024),
        cost_estimate=pl.CostEstimate(
            flops=rows * chans * 4, bytes_accessed=rows * chans * 10, transcendentals=0
        ),
        name=name,
    )(*flat, *rowed, *pieces)


def exchange(x):
    return lax.all_to_all(x, "seq", split_axis=0, concat_axis=0, tiled=True)


def local(
    hyena_gate, hyena_key, hyena_value, long_filter, skip_weight, attn_query, attn_keys, attn_values
):
    devices = lax.axis_size("seq")
    my_index = lax.axis_index("seq")
    rows, chans = hyena_key.shape
    each = chans // devices
    aligned = each % 128 == 0
    kv_pair = jnp.stack([attn_keys, attn_values])
    behind = lax.ppermute(kv_pair, "seq", [(i, i + 1) for i in range(devices - 1)])
    own = lax.all_gather(kv_pair, "chan", axis=2, tiled=True)
    if aligned:
        both = by_groups(
            prepare_kernel,
            (hyena_key, hyena_value, long_filter),
            (),
            (),
            (devices, 2 * rows, each),
            devices,
            "prepare",
        )
    else:
        signal = hyena_key.astype(jnp.float32) * hyena_value.astype(jnp.float32)
        both = jnp.concatenate([signal.astype(jnp.bfloat16), long_filter], axis=0)
        both = both.reshape(2 * rows, devices, each).transpose(1, 0, 2)
    behind, both = lax.optimization_barrier((behind, both))
    both = exchange(both)
    behind = lax.all_gather(behind, "chan", axis=2, tiled=True)
    tokens, groups, features = attn_query.shape
    queries = attn_query.reshape(tokens * groups, features)
    out, lse = attend(queries, groups, behind, own, my_index)
    out, lse, both = lax.optimization_barrier((out, lse, both))
    if aligned:
        conv = whole_conv(both)
        hyena_out = by_groups(
            finish_kernel,
            (hyena_gate, hyena_key, hyena_value),
            (skip_weight[None, :],),
            (exchange(conv),),
            (rows, chans),
            devices,
            "finish",
        )
    else:
        cube = (devices * rows // MINOR, MINOR, each)
        lines = 2 * cube[0]
        sig, ker = both[:, :rows].reshape(cube), both[:, rows:].reshape(cube)
        back = spectra_product(spread(sig), spread(ker), lines * MINOR)
        conv = gather_lines(*back, lines).astype(jnp.bfloat16)
        conv = exchange(conv.reshape(devices, rows, each)).transpose(1, 0, 2).reshape(rows, chans)
        signal = hyena_key.astype(jnp.float32) * hyena_value.astype(jnp.float32)
        hyena_out = hyena_gate.astype(jnp.float32) * (
            conv.astype(jnp.float32) + skip_weight * signal
        )
        hyena_out = hyena_out.astype(jnp.bfloat16)
    attn_lse = lse.reshape(features // HD, tokens, groups).transpose(2, 0, 1)
    return (hyena_out, out.reshape(attn_query.shape), attn_lse)


def solution(mesh):
    return jax.shard_map(
        local,
        mesh=mesh,
        in_specs=(
            P("seq", "chan"),
            P("seq", "chan"),
            P("seq", "chan"),
            P("seq", "chan"),
            P("chan"),
            P("seq", "chan", None),
            P("seq", "chan"),
            P("seq", "chan"),
        ),
        out_specs=(P("seq", "chan"), P("seq", "chan", None), P("chan", None, "seq")),
        check_vma=False,
    )
```

```python
import functools
import math

import jax
import jax.numpy as jnp
import numpy as np
from jax import lax
from jax.experimental import pallas as pl
from jax.experimental.pallas import tpu as pltpu
from jax.sharding import PartitionSpec as P

HD = 128
MINOR = 128
ROWS = 256
BIG = -1e30


def hi_lo(x):
    high = x.astype(jnp.bfloat16)
    return high, (x - high.astype(jnp.float32)).astype(jnp.bfloat16)


def split_table(table):
    high = table.astype(jnp.bfloat16)
    low = (table - high.astype(np.float64)).astype(jnp.bfloat16)
    return jnp.asarray(np.stack([high, low]))


def dot3(table_ref, x):
    high, low = hi_lo(x)
    total = jnp.dot(table_ref[0], high, preferred_element_type=jnp.float32)
    total += jnp.dot(table_ref[0], low, preferred_element_type=jnp.float32)
    return total + jnp.dot(table_ref[1], high, preferred_element_type=jnp.float32)


def class_kernel(fwd_ref, inv_ref, twist_ref, sr_ref, si_ref, kr_ref, ki_ref, out_re, out_im):
    for n in range(sr_ref.shape[0]):
        cos = twist_ref[n, :, 0:1]
        sin = twist_ref[n, :, 1:2]

        def spectrum(re, im):
            turned = jnp.concatenate([re * cos + im * sin, im * cos - re * sin], axis=0)
            return dot3(fwd_ref, turned)

        sig = spectrum(sr_ref[n], si_ref[n])
        ker = spectrum(kr_ref[n], ki_ref[n])
        s_re, s_im, k_re, k_im = sig[:MINOR], sig[MINOR:], ker[:MINOR], ker[MINOR:]
        prod = jnp.concatenate([s_re * k_re - s_im * k_im, s_re * k_im + s_im * k_re], axis=0)
        back = dot3(inv_ref, prod)
        b_re, b_im = back[:MINOR], back[MINOR:]
        out_re[n] = b_re * cos - b_im * sin
        out_im[n] = b_im * cos + b_re * sin


def spectra_product(sig, ker, span):
    classes, _, chans = sig[0].shape
    step = max(d for d in range(1, 6) if classes % d == 0)
    index = np.arange(MINOR)
    angle = 2 * math.pi / MINOR * (np.outer(index, index) % MINOR)
    cos, sin = np.cos(angle), np.sin(angle)
    fwd = split_table(np.block([[cos, sin], [-sin, cos]]))
    inv = split_table(np.block([[cos, -sin], [sin, cos]]))
    turn = 2 * math.pi / span * np.outer(np.arange(classes), index)
    twist = jnp.asarray(np.stack([np.cos(turn), np.sin(turn)], axis=-1), jnp.float32)
    table = pl.BlockSpec((2, 2 * MINOR, 2 * MINOR), lambda i: (0, 0, 0))
    block = pl.BlockSpec((step, MINOR, chans), lambda i: (i, 0, 0))
    shape = jax.ShapeDtypeStruct((classes, MINOR, chans), jnp.float32)
    return pl.pallas_call(
        class_kernel,
        grid=(classes // step,),
        in_specs=[table, table, pl.BlockSpec((step, MINOR, 2), lambda i: (i, 0, 0))] + [block] * 4,
        out_specs=[block, block],
        out_shape=[shape, shape],
        compiler_params=pltpu.CompilerParams(vmem_limit_bytes=40 * 1024 * 1024),
        cost_estimate=pl.CostEstimate(
            flops=classes * 18 * 4 * MINOR * MINOR * chans,
            bytes_accessed=classes * MINOR * chans * 24,
            transcendentals=0,
        ),
        name="class_products",
    )(fwd, inv, twist, *sig, *ker)


def line_tables(lines):
    classes = lines // 2 + 1
    angle = 2 * math.pi / lines * (np.outer(np.arange(classes), np.arange(lines // 2)) % lines)
    return np.cos(angle), np.sin(angle)


def spread(blocks):
    cos, sin = line_tables(2 * blocks.shape[0])
    wave = jnp.asarray(np.stack([cos, -sin]), jnp.float32)
    out = jnp.einsum(
        "rpk,kqc->rpqc", wave, blocks.astype(jnp.float32), precision=lax.Precision.HIGH
    )
    return out[0], out[1]


def gather_lines(re, im, lines):
    cos, sin = line_tables(lines)
    weight = np.full((lines // 2 + 1, 1), 2.0)
    weight[0] = weight[-1] = 1.0
    weight /= lines * MINOR
    cos = jnp.asarray((weight * cos).T, jnp.float32)
    sin = jnp.asarray((weight * sin).T, jnp.float32)
    out = jnp.einsum("tp,pqc->tqc", cos, re, precision=lax.Precision.HIGH)
    return out - jnp.einsum("tp,pqc->tqc", sin, im, precision=lax.Precision.HIGH)


def attend_kernel(groups, bias_ref, q_ref, kp_ref, vp_ref, ko_ref, vo_ref, out_ref, lse_ref):
    tokens = ko_ref.shape[1]
    tile = ROWS // groups
    scale = HD ** (-0.5)
    rate = scale * math.log2(math.e)
    bias = bias_ref[0, 0]
    v_before = vp_ref[0].T
    v_own = vo_ref[0].T
    key_row = lax.broadcasted_iota(jnp.int32, (tile, ROWS), 0)
    query_row = lax.broadcasted_iota(jnp.int32, (tile, ROWS), 1) // groups
    allowed = key_row <= query_row
    contract = functools.partial(
        lax.dot_general,
        dimension_numbers=(((1,), (1,)), ((), ())),
        preferred_element_type=jnp.float32,
    )
    for i in range(tokens // tile):
        rows = slice(i * ROWS, (i + 1) * ROWS)
        keys = (i + 1) * tile
        query = q_ref[rows, :]
        before = contract(kp_ref[0], query) + bias
        own = contract(ko_ref[0, :keys, :], query)
        last = jnp.where(allowed, own[keys - tile :], BIG)
        own = jnp.concatenate([own[: keys - tile], last], axis=0) if i else last
        peak = jnp.maximum(
            jnp.max(before, axis=0, keepdims=True), jnp.max(own, axis=0, keepdims=True)
        )
        before = jnp.exp2((before - peak) * rate)
        own = jnp.exp2((own - peak) * rate)
        total = jnp.sum(before, axis=0, keepdims=True) + jnp.sum(own, axis=0, keepdims=True)
        mixed = jnp.dot(
            v_before, before.astype(jnp.bfloat16), preferred_element_type=jnp.float32
        ) + jnp.dot(v_own[:, :keys], own.astype(jnp.bfloat16), preferred_element_type=jnp.float32)
        out_ref[rows, :] = (mixed * (1.0 / total)).T.astype(jnp.bfloat16)
        lse_ref[0, :, rows] = peak * scale + jnp.log(total)


def attend(queries, groups, behind, own, my_index):
    rows, features = queries.shape
    tokens = rows // groups
    heads = features // HD
    bias = jnp.where(my_index > 0, 0.0, BIG).astype(jnp.float32).reshape(1, 1)
    column = pl.BlockSpec((rows, HD), lambda j: (0, j))
    keys = pl.BlockSpec((1, tokens, HD), lambda j: (0, 0, j))
    values = pl.BlockSpec((1, tokens, HD), lambda j: (1, 0, j))
    return pl.pallas_call(
        functools.partial(attend_kernel, groups),
        grid=(heads,),
        in_specs=[
            pl.BlockSpec((1, 1), lambda j: (0, 0), memory_space=pltpu.SMEM),
            column,
            keys,
            values,
            keys,
            values,
        ],
        out_specs=[column, pl.BlockSpec((1, 1, rows), lambda j: (j, 0, 0))],
        out_shape=[
            jax.ShapeDtypeStruct((rows, features), jnp.bfloat16),
            jax.ShapeDtypeStruct((heads, 1, rows), jnp.float32),
        ],
        compiler_params=pltpu.CompilerParams(vmem_limit_bytes=40 * 1024 * 1024),
        cost_estimate=pl.CostEstimate(
            flops=heads * rows * 2 * tokens * HD * 4,
            bytes_accessed=rows * features * 4 + tokens * features * 8,
            transcendentals=heads * rows * 2 * tokens,
        ),
        name="attend",
    )(bias, queries, behind, behind, own, own)


def conv_kernel(w1_ref, w2_ref, fwd_ref, inv_ref, twist_ref, both_ref, out_ref, wide_ref, lines):
    devices, rows, chans = both_ref.shape
    half = wide_ref.shape[0] // MINOR
    both = w1_ref.shape[0]
    slots = both // 2
    kept = w2_ref.shape[1] // 6
    middle = chans // 2
    left = lax.broadcasted_iota(jnp.int32, (1, chans), 1) < middle
    swap = lambda x: pltpu.roll(x, middle, 1)

    def widen(i, _):
        at = pl.ds(pl.multiple_of(i * rows, rows), rows)
        wide_ref[at, :] = both_ref[i].astype(jnp.float32)
        return 0

    lax.fori_loop(0, devices, widen, 0)

    def first(i, _):
        cols = [wide_ref[pl.ds(2 * i + d, half, stride=MINOR), :] for d in range(2)]
        col = jnp.concatenate(cols, axis=1).astype(jnp.bfloat16)
        got = jnp.dot(
            w1_ref[...], jnp.concatenate([col, col], axis=0), preferred_element_type=jnp.float32
        )
        for d in range(2):
            at = pl.ds(pl.multiple_of((2 * i + d) * both, 8), both)
            lines[at, :] = got[:, d * chans : (d + 1) * chans]
        return 0

    lax.fori_loop(0, MINOR // 2, first, 0, unroll=4)

    def several(i, _):
        turned, turns = [], []
        for d in range(4):
            n = 4 * i + d
            re = lines[pl.ds(n, MINOR, stride=both), :]
            im = lines[pl.ds(n + slots, MINOR, stride=both), :]
            turn = twist_ref[n]
            cos, sin = turn[:, 0:1], turn[:, 1:2]
            turned.append(jnp.concatenate([re * cos + im * sin, im * cos - re * sin], axis=0))
            turns.append((cos, sin))
        prods = []
        for d in (0, 2):
            spec = dot3(fwd_ref, jnp.concatenate(turned[d : d + 2], axis=1))
            pair = []
            for x in (spec[:, :chans], spec[:, chans:]):
                y = swap(x)
                re, im, re2, im2 = x[:MINOR], x[MINOR:], y[:MINOR], y[MINOR:]
                pair.append(jnp.concatenate([re * re2 - im * im2, re * im2 + im * re2], axis=0))
            prods.append(jnp.where(left, pair[0], pair[1]))
        back = dot3(inv_ref, jnp.concatenate(prods, axis=1))
        for d in range(2):
            b_re = back[:MINOR, d * chans : (d + 1) * chans]
            b_im = back[MINOR:, d * chans : (d + 1) * chans]
            cos = jnp.where(left, turns[2 * d][0], turns[2 * d + 1][0])
            sin = jnp.where(left, turns[2 * d][1], turns[2 * d + 1][1])
            n = 2 * i + d
            lines[pl.ds(n, MINOR, stride=both), :] = b_re * cos - b_im * sin
            lines[pl.ds(n + slots, MINOR, stride=both), :] = b_im * cos + b_re * sin
        return 0

    lax.fori_loop(0, twist_ref.shape[0] // 4, several, 0)

    def last(i, _):
        cols = []
        for d in range(2):
            base = (i + d * (MINOR // 2)) * both
            cols.append(
                jnp.concatenate(
                    [
                        lines[pl.ds(pl.multiple_of(base, 8), kept), :],
                        lines[pl.ds(pl.multiple_of(base + slots, 8), kept), :],
                    ],
                    axis=0,
                )
            )
        high, low = hi_lo(jnp.concatenate(cols, axis=1))
        got = jnp.dot(
            w2_ref[...],
            jnp.concatenate([high, low, high], axis=0),
            preferred_element_type=jnp.float32,
        )
        early = got[:half, :chans] + swap(got[half:, :chans])
        late = swap(got[:half, chans:]) + got[half:, chans:]
        wide_ref[pl.ds(i, half, stride=MINOR // 2), :] = jnp.where(left, early, late)
        return 0

    lax.fori_loop(0, MINOR // 2, last, 0, unroll=4)

    def narrow(i, _):
        at = pl.ds(pl.multiple_of(i * (rows // 2), rows // 2), rows // 2)
        out_ref[i] = wide_ref[at, :].astype(jnp.bfloat16)
        return 0

    lax.fori_loop(0, devices, narrow, 0)


def whole_conv(both):
    devices, rows, chans = both.shape
    length = devices * rows
    half = length // MINOR
    lines, span = 2 * half, 2 * length
    classes = half + 1
    slots = -(-classes // 16) * 16
    cos, sin = line_tables(lines)
    w1 = np.zeros((2, slots, half))
    w1[0, :classes], w1[1, :classes] = cos, -sin
    w1 = split_table(w1.reshape(2 * slots, half))
    weight = np.full((classes, 1), 2.0)
    weight[0] = weight[-1] = 1.0
    weight /= span
    w2 = np.zeros((2, slots, half))
    w2[0, :classes], w2[1, :classes] = weight * cos, -weight * sin
    kept = -(-slots // 16) * 8
    paired = np.zeros((2, 2, kept, half))
    paired[:, :, : slots // 2] = w2.reshape(2, slots // 2, 2, half).transpose(2, 0, 1, 3)
    w2 = split_table(paired.transpose(0, 3, 1, 2).reshape(2 * half, 2 * kept))
    w1 = jnp.concatenate([w1[0], w1[1]], axis=1)
    w2 = jnp.concatenate([w2[0], w2[0], w2[1]], axis=1)
    index = np.arange(MINOR)
    angle = 2 * math.pi / MINOR * (np.outer(index, index) % MINOR)
    cos, sin = np.cos(angle), np.sin(angle)
    fwd = split_table(np.block([[cos, sin], [-sin, cos]]))
    inv = split_table(np.block([[cos, -sin], [sin, cos]]))
    turn = 2 * math.pi / span * np.outer(np.arange(-(-classes // 4) * 4), index)
    twist = jnp.asarray(np.stack([np.cos(turn), np.sin(turn)], axis=-1), jnp.float32)
    vmem = pl.BlockSpec(memory_space=pltpu.VMEM)
    return pl.pallas_call(
        conv_kernel,
        in_specs=[vmem] * 6,
        out_specs=vmem,
        out_shape=jax.ShapeDtypeStruct((devices, rows // 2, chans), jnp.bfloat16),
        scratch_shapes=[
            pltpu.VMEM((length, chans), jnp.float32),
            pltpu.VMEM((MINOR * 2 * slots, chans), jnp.float32),
        ],
        compiler_params=pltpu.CompilerParams(vmem_limit_bytes=48 * 1024 * 1024),
        cost_estimate=pl.CostEstimate(
            flops=classes * 18 * 4 * MINOR * MINOR * chans,
            bytes_accessed=length * chans * 6,
            transcendentals=0,
        ),
        name="whole_conv",
    )(w1, w2, fwd, inv, twist, both)


def prepare_kernel(key_ref, value_ref, filter_ref, *both_refs):
    each = both_refs[0].shape[2]
    for n in range(both_refs[0].shape[0]):
        for h, both_ref in enumerate(both_refs):
            at = slice(n * each + h * each // 2, n * each + (h + 1) * each // 2)
            signal = key_ref[:, at].astype(jnp.float32) * value_ref[:, at].astype(jnp.float32)
            both_ref[n] = jnp.concatenate(
                [signal, filter_ref[:, at].astype(jnp.float32)], axis=1
            ).astype(jnp.bfloat16)


def finish_kernel(gate_ref, key_ref, value_ref, skip_ref, one_ref, two_ref, out_ref):
    _, packed, each = one_ref.shape
    left = lax.broadcasted_iota(jnp.int32, (1, each), 1) < each // 2
    swap = lambda x: pltpu.roll(x, each // 2, 1)
    for n in range(one_ref.shape[0]):
        at = slice(n * each, (n + 1) * each)
        one, two = one_ref[n].astype(jnp.float32), two_ref[n].astype(jnp.float32)
        lows = jnp.where(left, one, swap(two)).reshape(-1, MINOR // 2, each)
        highs = jnp.where(left, swap(one), two).reshape(-1, MINOR // 2, each)
        conv = jnp.concatenate([lows, highs], axis=1).reshape(2 * packed, each)
        signal = key_ref[:, at].astype(jnp.float32) * value_ref[:, at].astype(jnp.float32)
        out = gate_ref[:, at].astype(jnp.float32) * (conv + skip_ref[:, at] * signal)
        out_ref[:, at] = out.astype(jnp.bfloat16)


def by_groups(kernel, flat, rowed, pieces, shape, devices, name):
    rows, chans = flat[0].shape
    each = chans // devices
    step = 4 if devices % 4 == 0 else 1
    whole = pl.BlockSpec((rows, step * each), lambda i: (0, i))
    thin = pl.BlockSpec((1, step * each), lambda i: (0, i))
    split = lambda n: pl.BlockSpec((step, n, each), lambda i: (i, 0, 0))
    out = jax.ShapeDtypeStruct(shape, jnp.bfloat16)
    return pl.pallas_call(
        kernel,
        grid=(devices // step,),
        in_specs=[whole] * len(flat) + [thin] * len(rowed) + [split(rows // 2)] * len(pieces),
        out_specs=whole if len(shape) == 2 else [split(rows)] * 2,
        out_shape=out if len(shape) == 2 else [out] * 2,
        compiler_params=pltpu.CompilerParams(vmem_limit_bytes=40 * 1024 * 1024),
        cost_estimate=pl.CostEstimate(
            flops=rows * chans * 4, bytes_accessed=rows * chans * 10, transcendentals=0
        ),
        name=name,
    )(*flat, *rowed, *pieces)


def exchange(x):
    return lax.all_to_all(x, "seq", split_axis=0, concat_axis=0, tiled=True)


def local(
    hyena_gate, hyena_key, hyena_value, long_filter, skip_weight, attn_query, attn_keys, attn_values
):
    devices = lax.axis_size("seq")
    my_index = lax.axis_index("seq")
    rows, chans = hyena_key.shape
    each = chans // devices
    aligned = each % 128 == 0
    kv_pair = jnp.stack([attn_keys, attn_values])
    behind = lax.ppermute(kv_pair, "seq", [(i, i + 1) for i in range(devices - 1)])
    own = lax.all_gather(kv_pair, "chan", axis=2, tiled=True)
    if aligned:
        both = by_groups(
            prepare_kernel,
            (hyena_key, hyena_value, long_filter),
            (),
            (),
            (devices, rows, each),
            devices,
            "prepare",
        )
    else:
        signal = hyena_key.astype(jnp.float32) * hyena_value.astype(jnp.float32)
        both = jnp.concatenate([signal.astype(jnp.bfloat16), long_filter], axis=0)
        both = [both.reshape(2 * rows, devices, each).transpose(1, 0, 2)]
    behind, both = lax.optimization_barrier((behind, both))
    both = [exchange(x) for x in both]
    behind = lax.all_gather(behind, "chan", axis=2, tiled=True)
    tokens, groups, features = attn_query.shape
    queries = attn_query.reshape(tokens * groups, features)
    queries, both[0] = lax.optimization_barrier((queries, both[0]))
    out, lse = attend(queries, groups, behind, own, my_index)
    out, lse, both[0] = lax.optimization_barrier((out, lse, both[0]))
    if aligned:
        conv = [whole_conv(x) for x in both]
        hyena_out = by_groups(
            finish_kernel,
            (hyena_gate, hyena_key, hyena_value),
            (skip_weight[None, :],),
            [exchange(x) for x in conv],
            (rows, chans),
            devices,
            "finish",
        )
    else:
        cube = (devices * rows // MINOR, MINOR, each)
        lines = 2 * cube[0]
        sig, ker = (x.reshape(cube) for x in (both[0][:, :rows], both[0][:, rows:]))
        back = spectra_product(spread(sig), spread(ker), lines * MINOR)
        conv = gather_lines(*back, lines).astype(jnp.bfloat16)
        conv = exchange(conv.reshape(devices, rows, each)).transpose(1, 0, 2).reshape(rows, chans)
        signal = hyena_key.astype(jnp.float32) * hyena_value.astype(jnp.float32)
        hyena_out = hyena_gate.astype(jnp.float32) * (
            conv.astype(jnp.float32) + skip_weight * signal
        )
        hyena_out = hyena_out.astype(jnp.bfloat16)
    attn_lse = lse.reshape(features // HD, tokens, groups).transpose(2, 0, 1)
    return (hyena_out, out.reshape(attn_query.shape), attn_lse)


def solution(mesh):
    return jax.shard_map(
        local,
        mesh=mesh,
        in_specs=(
            P("seq", "chan"),
            P("seq", "chan"),
            P("seq", "chan"),
            P("seq", "chan"),
            P("chan"),
            P("seq", "chan", None),
            P("seq", "chan"),
            P("seq", "chan"),
        ),
        out_specs=(P("seq", "chan"), P("seq", "chan", None), P("chan", None, "seq")),
        check_vma=False,
    )
```
